32 devices in a mesh: tok: 16 (over z, x, core), hid: 2 (over y).
Axes of the slice: x: 2, y: 2, z: 4, core: 2. Of those that a mesh axis runs over, the one named last changes fastest.
Arguments:
- base: float32 [512, 16384], P('tok', 'hid'), may hold values from -6 to 6
- source: float32 [512, 16384], P('tok', 'hid'), may hold values from -6 to 6
- pairs: int32 [512], replicated, may hold values from 0 to 511, each once
- counts: int32 [512], replicated, may hold values from 1 to 128
- rotation: float32 [16384, 16384], P('hid', 'tok'), may hold values from -0.046875 to 0.046875
Outputs:
- patched: float32 [512, 16384], P('tok', 'hid')
The draws below stay inside these ranges and needn't reach their ends.
All inputs are finite; a program needn't handle non-finite values.
Results may differ from the reference program's by a relative error of at most 0.000075.
Values sent between devices are 32-bit elements; how exact they have to be, the bound alone decides.
A program may use at most 128 MiB of HBM per device.

```python
import jax
import jax.numpy as jnp
from jax import lax

D = 16384
BLOCK = 128
ROWS = 512


def set_ends(drawn, rng, smallest, high):
    longest = drawn.shape.index(max(drawn.shape))
    spots = []
    for shift in (0, 1):
        where = [jax.random.randint(jax.random.fold_in(rng, axis), (), 0, length) for axis, length in enumerate(drawn.shape)]
        where[longest] = (where[longest] + shift) % drawn.shape[longest]
        spots.append(tuple(where))
    return drawn.at[spots[0]].set(smallest).at[spots[1]].set(high)


def shard_levels(rng, dims, cuts, smallest, top_value):
    level = 1.0
    for position, blocks in cuts:
        steps = jax.random.uniform(jax.random.fold_in(jax.random.fold_in(rng, 6), position), (blocks,), jnp.float32, smallest / len(cuts), top_value / len(cuts))
        level = level * jnp.repeat(jnp.exp(steps), dims[position] // blocks).reshape((-1,) + (1,) * (len(dims) - 1 - position))
    return level


def scatter_about(key, shape, deviation, limit, shards=(), held_as=jnp.bfloat16):
    factor_of = shard_levels(key, shape, shards, -0.22, 0.18) if shards else 1.0
    drawn = jax.random.normal(key, shape, jnp.float32) * deviation * factor_of
    return jnp.minimum(jnp.maximum(drawn, -limit), limit).astype(held_as)


def setup_inputs(seed: int = 0) -> dict:
    key_of = jax.random.split(jax.random.key(seed), 6)
    return {
        "base": scatter_about(key_of[0], (ROWS, D), 1.0, 6.0, ((0, 16), (1, 2)), jnp.float32),
        "source": scatter_about(key_of[1], (ROWS, D), 1.0, 6.0, ((0, 16), (1, 2)), jnp.float32),
        "pairs": jax.random.permutation(key_of[2], ROWS).astype(jnp.int32),
        "counts": set_ends(jax.random.randint(key_of[3], (ROWS,), 1, D // BLOCK + 1), jax.random.fold_in(key_of[3], 1), 1, (D // BLOCK + 1) - 1).astype(jnp.int32),
        "rotation": scatter_about(key_of[4], (D, D), D ** -0.5, 0.046875, ((0, 2), (1, 16)), jnp.float32),
    }


def reference(base, source, pairs, counts, rotation):
    highest = lax.Precision.HIGHEST
    rotated_base = jnp.dot(base, rotation, precision=highest, preferred_element_type=jnp.float32)
    paired = jnp.take(source, pairs.astype(jnp.int32), axis=0)
    rotated_source = jnp.dot(paired, rotation, precision=highest, preferred_element_type=jnp.float32)
    columns = jnp.arange(D, dtype=jnp.int32)
    limits = counts.astype(jnp.int32) * BLOCK
    mixed = jnp.where(columns[None, :] < limits[:, None], rotated_source, rotated_base)
    return lax.dot_general(mixed, rotation, (((1,), (1,)), ((), ())), precision=highest, preferred_element_type=jnp.float32)
```

```python
import jax
import jax.numpy as jnp
from jax import lax
from jax.sharding import PartitionSpec as P

BLOCK = 128
K_PARTS = 4
ROW_PARTS = 4


def product(left, right, contract):
    return lax.dot_general(
        left,
        right,
        (contract, ((), ())),
        precision=lax.Precision.HIGH,
        preferred_element_type=jnp.float32,
    )


def local(tok, hid, base, source, pairs, counts, rotation):
    held, depth = base.shape
    width = rotation.shape[1]
    me = lax.axis_index("tok")
    core = lax.rem(me, 2)

    stacked = jnp.concatenate([base, source], axis=0)
    step = depth // K_PARTS
    terms = None
    for part in range(K_PARTS):
        rows = lax.all_gather(
            stacked[:, part * step : (part + 1) * step], "tok", axis=0, tiled=True
        )
        term = product(rows, rotation[part * step : (part + 1) * step], ((1,), (0,)))
        terms = term if terms is None else terms + term

    columns = me * width + jnp.arange(width, dtype=jnp.int32)
    share = held // ROW_PARTS
    chips = jnp.arange(tok // 2, dtype=jnp.int32)[:, None]
    within = jnp.arange(share, dtype=jnp.int32)[None, :]
    siblings = [(t, t ^ 1) for t in range(tok)]
    groups = [list(range(c, tok, 2)) for c in range(2)]

    def mix(part):
        index = jnp.concatenate(
            [
                ((chips * 2 + c) * held + part * share + within).reshape(-1)
                for c in (1 - core, core)
            ]
        )
        pair = pairs[index]
        base_at = (index // held) * (2 * held) + index % held
        source_at = (pair // held) * (2 * held) + held + pair % held
        limits = counts[index] * BLOCK
        return jnp.where(
            columns[None, :] < limits[:, None],
            terms.at[source_at].get(mode="promise_in_bounds"),
            terms.at[base_at].get(mode="promise_in_bounds"),
        )

    def summed_over_hid(mixed):
        if hid != 2:
            return lax.psum(mixed, "hid")
        return mixed + lax.ppermute(mixed, "hid", [(0, 1), (1, 0)])

    outs = []
    for part in range(ROW_PARTS):
        full = summed_over_hid(mix(part))
        partial = product(full, rotation, ((1,), (1,)))
        half = partial.shape[0] // 2
        mine = partial[half:] + lax.ppermute(partial[:half], "tok", siblings)
        outs.append(
            lax.psum_scatter(
                mine, "tok", scatter_dimension=0, axis_index_groups=groups, tiled=True
            )
        )
    return jnp.concatenate(outs, axis=0)


def solution(mesh):
    tok, hid = mesh.shape["tok"], mesh.shape["hid"]

    def run(*args):
        return local(tok, hid, *args)

    return jax.shard_map(
        run,
        mesh=mesh,
        in_specs=(P("tok", "hid"), P("tok", "hid"), P(), P(), P("hid", "tok")),
        out_specs=P("tok", "hid"),
        check_vma=False,
    )
```

```python
import jax
import jax.numpy as jnp
from jax import lax
from jax.sharding import PartitionSpec as P

BLOCK = 128


def split(x):
    high = lax.reduce_precision(x, exponent_bits=8, mantissa_bits=7)
    return high.astype(jnp.bfloat16), (x - high).astype(jnp.bfloat16)


def product(left, right, contract):
    rows = left.shape[0]
    high, low = split(left)

    def dot(a, b):
        return lax.dot_general(
            a, b, (contract, ((), ())), preferred_element_type=jnp.float32
        )

    both = dot(jnp.concatenate([high, low], axis=0), right[0])
    return both[:rows] + (both[rows:] + dot(high, right[1]))


def local(tok, hid, base, source, pairs, counts, rotation):
    held, depth = base.shape
    width = rotation.shape[1]
    me = lax.axis_index("tok")
    core = lax.rem(me, 2)
    n = tok // 2

    order = list(range(0, n, 2)) + list(range(1, n, 2))[::-1]
    up = [
        (order[i] * 2 + c, order[(i + 1) % n] * 2 + c) for i in range(n) for c in (0, 1)
    ]
    down = [(b, a) for a, b in up]
    siblings = [(t, t ^ 1) for t in range(tok)]

    def place(chip):
        return jnp.where(chip % 2 == 0, chip // 2, n - 1 - chip // 2)

    def chip_at(position):
        return jnp.where(position * 2 < n, position * 2, (n - 1 - position) * 2 + 1)

    here = place(me // 2)

    weights = lax.optimization_barrier(split(rotation))

    terms, ready = [], []
    a, b = base, source
    for step in range(n):
        if step < n - 1:
            next_a = lax.ppermute(a, "tok", up)
            next_b = lax.ppermute(b, "tok", down)
        mine = jnp.concatenate([a, b], axis=0)
        other = lax.ppermute(mine, "tok", siblings)
        ready.append(jnp.concatenate([mine, other], axis=0))
        if step > 0:
            terms.append(product(ready[step - 1], weights, ((1,), (0,))))
        if step < n - 1:
            if step > 0:
                a, b, ready[step], terms[-1] = lax.optimization_barrier(
                    (next_a, next_b, ready[step], terms[-1])
                )
            else:
                a, b, ready[0], *weights = lax.optimization_barrier(
                    (next_a, next_b, ready[0], *weights)
                )
    terms.append(product(ready[n - 1], weights, ((1,), (0,))))
    terms = jnp.concatenate(terms, axis=0)

    def base_at(row):
        owner = row // held
        step = (here - place(owner // 2) + n) % n
        return step * 4 * held + (owner % 2 != core) * 2 * held + row % held

    def source_at(row):
        owner = row // held
        step = (place(owner // 2) - here + n) % n
        return step * 4 * held + (owner % 2 != core) * 2 * held + held + row % held

    columns = me * width + jnp.arange(width, dtype=jnp.int32)
    share = held // 2
    within = jnp.arange(share, dtype=jnp.int32)

    def rows_of(step):
        first = chip_at((here - 1 - step + 2 * n) % n)
        second = chip_at((here + 1 + step) % n)
        return [
            jnp.concatenate(
                [
                    (first * 2 + c) * held + within,
                    (second * 2 + c) * held + share + within,
                ]
            )
            for c in (core, 1 - core)
        ]

    def summed_over_hid(mixed):
        if hid != 2:
            return lax.psum(mixed, "hid")
        return mixed + lax.ppermute(mixed, "hid", [(0, 1), (1, 0)])

    group = 2
    parts = []
    for first in range(0, n, group):
        lists = [rows_of(first + i) for i in range(group)]
        index = jnp.concatenate([l[0] for l in lists] + [l[1] for l in lists])
        limits = counts[index] * BLOCK
        mixed = jnp.where(
            columns[None, :] < limits[:, None],
            terms.at[source_at(pairs[index])].get(mode="promise_in_bounds"),
            terms.at[base_at(index)].get(mode="promise_in_bounds"),
        )
        parts.append(summed_over_hid(mixed))

    def summed_over_cores(partial):
        half = partial.shape[0] // 2
        return partial[:half] + lax.ppermute(partial[half:], "tok", siblings)

    a = b = None
    mine = summed_over_cores(product(parts[0], weights, ((1,), (1,))))
    for number in range(len(parts)):
        later = None
        if number + 1 < len(parts):
            mine, full = lax.optimization_barrier((mine, parts[number + 1]))
            later = product(full, weights, ((1,), (1,)))
        for i in range(group):
            here_a = mine[2 * i * share : (2 * i + 1) * share]
            here_b = mine[(2 * i + 1) * share : (2 * i + 2) * share]
            a = here_a if a is None else here_a + a
            b = here_b if b is None else here_b + b
            if number * group + i < n - 1:
                a = lax.ppermute(a, "tok", up)
                b = lax.ppermute(b, "tok", down)
                if i == 0 and later is not None:
                    a, b, later = lax.optimization_barrier((a, b, later))
                else:
                    a, b = lax.optimization_barrier((a, b))
        if later is not None:
            mine = summed_over_cores(later)
    return jnp.concatenate([a, b], axis=0)


def solution(mesh):
    tok, hid = mesh.shape["tok"], mesh.shape["hid"]

    def run(*args):
        return local(tok, hid, *args)

    return jax.shard_map(
        run,
        mesh=mesh,
        in_specs=(P("tok", "hid"), P("tok", "hid"), P(), P(), P("hid", "tok")),
        out_specs=P("tok", "hid"),
        check_vma=False,
    )
```
